768 devices in a mesh: island: 4 (over z_hi), fsdp: 192 (over z_lo, y, x, core).
Axes of the slice: x: 4, y: 8, z: 12 (z_hi: 4, z_lo: 3; z = z_hi * 3 + z_lo), core: 2. Of those that a mesh axis runs over, the one named last changes fastest.
Arguments:
- normed_input: bfloat16 [4, 73728, 4608], P('island', 'fsdp'), may hold values from -24 to 24
- kv_cotangent: bfloat16 [4, 73728, 512], P('island', 'fsdp'), may hold values from -6 to 6
- kv_weight: float32 [4, 4608, 512], P('island', 'fsdp'), may hold values from -6 to 6
- adam_m: float32 [4, 4608, 512], P('island', 'fsdp'), may hold values from -6 to 6
- adam_v: float32 [4, 4608, 512], P('island', 'fsdp'), may hold values from 0.25 to 4
- outer_params: float32 [2, 3145728], P(None, 'fsdp'), may hold values from -6 to 6
- local_params: float32 [4, 2, 3145728], P('island', None, 'fsdp'), may hold values from -6 to 6
- outer_momentum: float32 [2, 3145728], P(None, 'fsdp'), may hold values from -6 to 6
- fragment: int32 [1], replicated, may hold values from 0 to 1
- block_exponent: int32 [24576], P('fsdp'), may hold values from 0 to 9
Outputs:
- new_weight: float32 [4, 4608, 512], P('island', 'fsdp')
- new_m: float32 [4, 4608, 512], P('island', 'fsdp')
- new_v: float32 [4, 4608, 512], P('island', 'fsdp')
- new_outer: float32 [2, 3145728], P(None, 'fsdp')
- new_momentum: float32 [2, 3145728], P(None, 'fsdp')
- new_local: float32 [4, 2, 3145728], P('island', None, 'fsdp')
The draws below stay inside these ranges and needn't reach their ends.
All inputs are finite; a program needn't handle non-finite values.
Results may differ from the reference program's by a relative error of at most 0.0018.
Values may be sent and summed in bfloat16 or wider, within the bound.
No kernel may reach another device: no remote copies, remote signals or barrier semaphores. Data moves between devices by JAX's collectives and lax.ppermute only.
A program may use at most 32 MiB of HBM per device.

```python
import math
import jax
import jax.numpy as jnp
from jax import lax

D = 4608
PAIR = 512
TOKENS = 73728
ISLANDS = 4
FRAG = 3145728
FRAGS = 2
BLOCK = 128


def plant(entries, rng, low, high):
    longest = entries.shape.index(max(entries.shape))
    spots = []
    for shift in (0, 1):
        where = [jax.random.randint(jax.random.fold_in(rng, axis), (), 0, length) for axis, length in enumerate(entries.shape)]
        where[longest] = (where[longest] + shift) % entries.shape[longest]
        spots.append(tuple(where))
    return entries.at[spots[0]].set(low).at[spots[1]].set(high)


def spiked(entries, stream_key, source, target, blocks, factor):
    owner, partner = [(jnp.arange(entries.shape[position]) // (entries.shape[position] // blocks)).reshape([-1 if axis == position else 1 for axis in range(entries.ndim)]) for position in (source, target)]
    chosen = jax.random.permutation(stream_key, blocks)[partner]
    strong = (owner == chosen) | (owner == (partner + blocks // 2) % blocks)
    return jnp.where(strong, factor * entries, entries)


def levels(own_key, shape, split, low, high):
    def one(dim, parts):
        heights = jax.random.uniform(jax.random.fold_in(jax.random.fold_in(own_key, 6), dim), (parts,), jnp.float32, low / len(split), high / len(split))
        return jnp.repeat(jnp.exp(heights), shape[dim] // parts).reshape((-1,) + (1,) * (len(shape) - dim - 1))

    gain = one(*split[0])
    for cut in split[1:]:
        gain = gain * one(*cut)
    return gain


def gaussian(key, shape, width, bound, shards=(), held_as=jnp.bfloat16):
    values = width * jax.random.normal(key, shape, jnp.float32)
    if shards:
        values = values * levels(key, shape, shards, -0.22, 0.18)
    return jnp.clip(values, -bound, bound).astype(held_as)


def bell_draw_with(stream_key, extent, deviation, reach, pieces, heavy, held_as=jnp.bfloat16):
    drawn = deviation * jax.random.normal(stream_key, extent, jnp.float32)
    if pieces:
        drawn = drawn * levels(stream_key, extent, pieces, -0.22, 0.18)
    return jnp.clip(spiked(drawn, jax.random.fold_in(stream_key, 3), *heavy), -reach, reach).astype(held_as)


def setup_inputs(seed: int = 0) -> dict:
    key_of = jax.random.split(jax.random.key(seed), 11)
    normed_input = bell_draw_with(key_of[0], (ISLANDS, TOKENS, D), 1.0, 24.0, ((0, 4), (1, 192)), (1, 2, 192, 6.0))
    kv_cotangent = gaussian(key_of[1], (ISLANDS, TOKENS, PAIR), 1.0, 6.0, ((0, 4), (1, 192)))
    kv_weight = gaussian(key_of[2], (ISLANDS, D, PAIR), 1.0, 6.0, ((0, 4), (1, 192)), jnp.float32)
    adam_m = gaussian(key_of[3], (ISLANDS, D, PAIR), 1.0, 6.0, ((0, 4), (1, 192)), jnp.float32)
    adam_v = jnp.clip(jnp.exp(math.log(4.0) - 2.7725887 * jax.random.uniform(key_of[4], (ISLANDS, D, PAIR), jnp.float32) ** levels(key_of[4], (ISLANDS, D, PAIR), ((0, 4), (1, 192)), -0.2, 0.2)), 0.25, 4.0)
    outer_params = gaussian(key_of[5], (FRAGS, FRAG), 1.0, 6.0, ((1, 192),), jnp.float32)
    local_params = gaussian(key_of[6], (ISLANDS, FRAGS, FRAG), 1.0, 6.0, ((0, 4), (2, 192)), jnp.float32)
    outer_momentum = gaussian(key_of[7], (FRAGS, FRAG), 1.0, 6.0, ((1, 192),), jnp.float32)
    fragment = jax.random.randint(key_of[8], (1,), 0, FRAGS).astype(jnp.int32)
    block_exponent = plant(jax.random.randint(key_of[9], (FRAG // BLOCK,), 0, 10), jax.random.fold_in(key_of[9], 1), 0, 9).astype(jnp.int32)
    return {"normed_input": normed_input, "kv_cotangent": kv_cotangent, "kv_weight": kv_weight, "adam_m": adam_m, "adam_v": adam_v, "outer_params": outer_params, "local_params": local_params, "outer_momentum": outer_momentum, "fragment": fragment, "block_exponent": block_exponent}


beta_one = 0.9
beta_two = 0.95
bias_one = 1.0 - 0.9 ** 10
bias_two = 1.0 - 0.95 ** 10
adam_eps = 1e-08
decay_rate = 0.1
inner_rate = 0.01
outer_rate = 0.7
momentum_coef = 0.9
mixing_alpha = 0.5
code_limit = 448.0

def adamw_step(weight, first, second, gradient):
    first_new = beta_one * first + (1.0 - beta_one) * gradient
    second_new = beta_two * second + (1.0 - beta_two) * gradient * gradient
    update = first_new / bias_one / (jnp.sqrt(second_new / bias_two) + adam_eps) + decay_rate * weight
    return (weight - inner_rate * update, first_new, second_new)

def reference(normed_input, kv_cotangent, kv_weight, adam_m, adam_v, outer_params, local_params, outer_momentum, fragment, block_exponent):
    weights, firsts, seconds = ([], [], [])
    for island in range(ISLANDS):
        gradient = lax.dot_general(normed_input[island], kv_cotangent[island], (((0,), (0,)), ((), ())), preferred_element_type=jnp.float32) / math.sqrt(TOKENS)
        weight_new, first_new, second_new = adamw_step(kv_weight[island], adam_m[island], adam_v[island], gradient)
        weights.append(weight_new)
        firsts.append(first_new)
        seconds.append(second_new)
    frag_index = fragment[0]
    outer_now = lax.dynamic_index_in_dim(outer_params, frag_index, 0, keepdims=False).reshape(-1, BLOCK)
    moment_now = lax.dynamic_index_in_dim(outer_momentum, frag_index, 0, keepdims=False).reshape(-1, BLOCK)
    block_scale = jnp.exp2(block_exponent.astype(jnp.float32))[:, None]
    summed = jnp.zeros(outer_now.shape, jnp.float32)
    locals_now = []
    for island in range(ISLANDS):
        local_now = lax.dynamic_index_in_dim(local_params[island], frag_index, 0, keepdims=False).reshape(-1, BLOCK)
        locals_now.append(local_now)
        encoded = jnp.clip((outer_now - local_now) * block_scale, -code_limit, code_limit).astype(jnp.bfloat16)
        encoded = lax.optimization_barrier(encoded)
        summed = summed + encoded.astype(jnp.float32)
    pseudo = summed / block_scale / ISLANDS
    moment_new = momentum_coef * moment_now + pseudo
    outer_new = outer_now - outer_rate * (pseudo + momentum_coef * moment_new)
    new_outer = lax.dynamic_update_index_in_dim(outer_params, outer_new.reshape(-1), frag_index, 0)
    new_momentum = lax.dynamic_update_index_in_dim(outer_momentum, moment_new.reshape(-1), frag_index, 0)
    mixed = []
    for island in range(ISLANDS):
        merged = (mixing_alpha * locals_now[island] + (1.0 - mixing_alpha) * outer_new).reshape(-1)
        mixed.append(lax.dynamic_update_index_in_dim(local_params[island], merged, frag_index, 0))
    return (jnp.stack(weights), jnp.stack(firsts), jnp.stack(seconds), new_outer, new_momentum, jnp.stack(mixed))
```

```python
import math

import jax
import jax.numpy as jnp
from jax import lax
from jax.sharding import Mesh
from jax.sharding import PartitionSpec as P

FSDP = ("z", "y", "x", "core")

beta_one = 0.9
beta_two = 0.95
bias_one = 1.0 - 0.9**10
bias_two = 1.0 - 0.95**10
adam_eps = 1e-08
decay_rate = 0.1
inner_rate = 0.01
outer_rate = 0.7
momentum_coef = 0.9
mixing_alpha = 0.5
code_limit = 448.0


def adamw_step(weight, first, second, gradient):
    first_new = beta_one * first + (1.0 - beta_one) * gradient
    second_new = beta_two * second + (1.0 - beta_two) * gradient * gradient
    update = (
        first_new / bias_one / (jnp.sqrt(second_new / bias_two) + adam_eps) + decay_rate * weight
    )
    return (weight - inner_rate * update, first_new, second_new)


def other_core(partial):
    there = 1 - lax.axis_index("core")
    leaving = lax.dynamic_index_in_dim(partial, there, 1, keepdims=False)
    return lax.ppermute(leaving, "core", [(0, 1), (1, 0)])


def along_x(piece_of, size):
    here = lax.axis_index("x")
    total = piece_of(here)
    for step in range(1, size):
        leaving = piece_of(lax.rem(here + step, size)).astype(jnp.bfloat16)
        arrived = lax.ppermute(leaving, "x", [(i, (i + step) % size) for i in range(size)])
        total = total + arrived.astype(jnp.float32)
    return total


def along_zy(pieces):
    arrived = lax.all_to_all(pieces.astype(jnp.bfloat16), ("z", "y"), 0, 0, tiled=True)
    return jnp.sum(arrived.astype(jnp.float32), axis=0)


def inner_step(normed_input, kv_cotangent, kv_weight, adam_m, adam_v):
    inputs_here = normed_input[0]
    cotangent_here = kv_cotangent[0]
    rows, columns = kv_weight.shape[1:]
    nx, nzy, cores = lax.axis_size("x"), lax.axis_size(("z", "y")), lax.axis_size("core")
    island_tokens = inputs_here.shape[0] * nx * nzy * cores
    norm_factor = math.sqrt(island_tokens)
    core = lax.axis_index("core")
    cut = columns * 3 // 4

    product = lax.dot_general(
        inputs_here, cotangent_here, (((0,), (0,)), ((), ())), preferred_element_type=jnp.float32
    )
    product = product.astype(jnp.bfloat16).reshape(nzy * nx, cores, rows, columns)

    wide, narrow = product[..., :cut], product[..., cut:]
    wide_other, narrow_other = other_core(wide), other_core(narrow)

    def wide_piece(owner):
        mine = wide.reshape(nzy, nx, cores, rows, cut)
        mine = lax.dynamic_slice(mine, (0, owner, core, 0, 0), (nzy, 1, 1, rows, cut))
        other = lax.dynamic_index_in_dim(
            wide_other.reshape(nzy, nx, rows, cut), owner, 1, keepdims=False
        )
        return mine.reshape(nzy, rows, cut).astype(jnp.float32) + other.astype(jnp.float32)

    narrow_mine = lax.dynamic_index_in_dim(narrow, core, 1, keepdims=False)
    narrow_sum = narrow_mine.astype(jnp.float32) + narrow_other.astype(jnp.float32)
    narrow_sum = along_zy(narrow_sum.reshape(nzy, nx, rows, -1))
    narrow_sum = lax.optimization_barrier(narrow_sum)
    narrow_sum = along_x(
        lambda owner: lax.dynamic_index_in_dim(narrow_sum, owner, 0, keepdims=False), nx
    )
    wide_sum = along_zy(along_x(wide_piece, nx))
    summed = jnp.concatenate([wide_sum, narrow_sum], axis=1)
    weight_new, first_new, second_new = adamw_step(
        kv_weight[0], adam_m[0], adam_v[0], summed / norm_factor
    )
    return (weight_new[None], first_new[None], second_new[None])


def nesterov_update(outer_part, moment_part, pseudo):
    moment_new = momentum_coef * moment_part + pseudo
    outer_new = outer_part - outer_rate * (pseudo + momentum_coef * moment_new)
    return (outer_new, moment_new)


def outer_step(outer_params, local_params, outer_momentum, fragment, block_exponent):
    second = fragment[0] == 1
    blocks = block_exponent.shape[0]
    fragments, length = outer_params.shape
    chosen = lax.broadcasted_iota(jnp.int32, (fragments, length), 0) == fragment[0]

    def pick(both):
        return jnp.where(second, both[1], both[0]).reshape(blocks, -1)

    def put(both, new):
        return jnp.where(chosen, new.reshape(1, length), both)

    outer_now, moment_now, local_now = pick(outer_params), pick(outer_momentum), pick(local_params[0])
    block_scale = jnp.exp2(block_exponent.astype(jnp.float32))[:, None]
    encoded = jnp.clip((outer_now - local_now) * block_scale, -code_limit, code_limit).astype(
        jnp.bfloat16
    )
    islands = lax.axis_size("island")
    copies = jnp.broadcast_to(encoded[None], (islands,) + encoded.shape)
    gathered = lax.all_to_all(copies, "island", 0, 0, tiled=True)
    summed = jnp.sum(gathered.astype(jnp.float32), axis=0)
    pseudo = summed / block_scale / islands
    outer_new, moment_new = nesterov_update(outer_now, moment_now, pseudo)
    merged = mixing_alpha * local_now + (1.0 - mixing_alpha) * outer_new
    return (put(outer_params, outer_new), put(outer_momentum, moment_new), put(local_params[0], merged)[None])


def on_device(
    normed_input,
    kv_cotangent,
    kv_weight,
    adam_m,
    adam_v,
    outer_params,
    local_params,
    outer_momentum,
    fragment,
    block_exponent,
):
    inner_result = inner_step(normed_input, kv_cotangent, kv_weight, adam_m, adam_v)
    outer_result = outer_step(outer_params, local_params, outer_momentum, fragment, block_exponent)
    return (
        inner_result[0],
        inner_result[1],
        inner_result[2],
        outer_result[0],
        outer_result[1],
        outer_result[2],
    )


def solution(mesh):
    grid = Mesh(mesh.devices.reshape(mesh.shape["island"], 3, 8, 4, 2), ("island",) + FSDP)
    in_specs = (
        P("island", FSDP, None),
        P("island", FSDP, None),
        P("island", FSDP, None),
        P("island", FSDP, None),
        P("island", FSDP, None),
        P(None, FSDP),
        P("island", None, FSDP),
        P(None, FSDP),
        P(),
        P(FSDP),
    )
    out_specs = (
        P("island", FSDP, None),
        P("island", FSDP, None),
        P("island", FSDP, None),
        P(None, FSDP),
        P(None, FSDP),
        P("island", None, FSDP),
    )
    return jax.shard_map(
        on_device, mesh=grid, in_specs=in_specs, out_specs=out_specs, check_vma=False
    )
```

```python
import functools
import math

import jax
import jax.numpy as jnp
from jax import lax
from jax.experimental import pallas as pl
from jax.experimental.pallas import tpu as pltpu
from jax.sharding import Mesh
from jax.sharding import PartitionSpec as P

FSDP = ("z", "y", "x", "core")

beta_one = 0.9
beta_two = 0.95
bias_one = 1.0 - 0.9**10
bias_two = 1.0 - 0.95**10
adam_eps = 1e-08
decay_rate = 0.1
inner_rate = 0.01
outer_rate = 0.7
momentum_coef = 0.9
mixing_alpha = 0.5
code_limit = 448.0


def adamw_step(weight, first, second, gradient):
    first_new = beta_one * first + (1.0 - beta_one) * gradient
    second_new = beta_two * second + (1.0 - beta_two) * gradient * gradient
    update = (
        first_new / bias_one / (jnp.sqrt(second_new / bias_two) + adam_eps) + decay_rate * weight
    )
    return (weight - inner_rate * update, first_new, second_new)


def product_kernel(inputs, cotangent, leaving, staying, *, rows):
    product = lax.dot_general(
        inputs[...], cotangent[...], (((0,), (0,)), ((), ())), preferred_element_type=jnp.float32
    )
    product = product.reshape(-1, 2, rows, product.shape[-1])
    first = product[:, 0].reshape(leaving.shape).astype(jnp.bfloat16)
    second = product[:, 1].reshape(leaving.shape).astype(jnp.bfloat16)
    core = lax.axis_index("core")

    @pl.when(core == 0)
    def _():
        staying[...] = first
        leaving[...] = second

    @pl.when(core == 1)
    def _():
        staying[...] = second
        leaving[...] = first


def product_by_core(inputs, cotangent, rows):
    tokens, wide = inputs.shape
    columns = cotangent.shape[1]
    block = wide // 2
    half = jax.ShapeDtypeStruct((wide // 2, columns), jnp.bfloat16)
    out_spec = pl.BlockSpec((block // 2, columns), lambda i: (i, 0))
    return pl.pallas_call(
        functools.partial(product_kernel, rows=rows),
        grid=(wide // block,),
        in_specs=[
            pl.BlockSpec((tokens, block), lambda i: (0, i)),
            pl.BlockSpec((tokens, columns), lambda i: (0, 0)),
        ],
        out_specs=[out_spec, out_spec],
        out_shape=[half, half],
        compiler_params=pltpu.CompilerParams(vmem_limit_bytes=58 * 1024 * 1024),
        cost_estimate=pl.CostEstimate(
            flops=2 * tokens * wide * columns,
            bytes_accessed=2 * (tokens * (wide + columns) + wide * columns),
            transcendentals=0,
        ),
    )(inputs, cotangent)


def inner_sum(staying, arrived, rows):
    pair = staying.astype(jnp.float32) + arrived.astype(jnp.float32)
    return pair.astype(jnp.bfloat16).reshape(-1, rows, staying.shape[-1])


def nesterov_update(outer_part, moment_part, pseudo):
    moment_new = momentum_coef * moment_part + pseudo
    outer_new = outer_part - outer_rate * (pseudo + momentum_coef * moment_new)
    return (outer_new, moment_new)


def pick(both, fragment, blocks):
    return jnp.where(fragment[0] == 1, both[1], both[0]).reshape(blocks, -1)


def put(both, fragment, new):
    chosen = lax.broadcasted_iota(jnp.int32, both.shape, 0) == fragment[0]
    return jnp.where(chosen, new.reshape(1, -1), both)


def encode(outer_params, local_params, fragment, block_scale):
    blocks = block_scale.shape[0]
    change = pick(outer_params, fragment, blocks) - pick(local_params, fragment, blocks)
    return jnp.clip(change * block_scale, -code_limit, code_limit).astype(jnp.bfloat16)


def outer_step(pair, other_pair, outer_params, local_params, outer_momentum, fragment, block_scale):
    blocks = block_scale.shape[0]
    pair, other_pair = pair.astype(jnp.float32), other_pair.astype(jnp.float32)
    summed = (pair[0] + pair[1]) + (other_pair[0] + other_pair[1])
    pseudo = summed / block_scale / lax.axis_size("island")
    outer_now, moment_now, local_now = (
        pick(both, fragment, blocks) for both in (outer_params, outer_momentum, local_params)
    )
    outer_new, moment_new = nesterov_update(outer_now, moment_now, pseudo)
    merged = mixing_alpha * local_now + (1.0 - mixing_alpha) * outer_new
    return (
        put(outer_params, fragment, outer_new),
        put(outer_momentum, fragment, moment_new),
        put(local_params, fragment, merged)[None],
    )


def on_device(
    normed_input,
    kv_cotangent,
    kv_weight,
    adam_m,
    adam_v,
    outer_params,
    local_params,
    outer_momentum,
    fragment,
    block_exponent,
):
    inputs_here, cotangent_here = normed_input[0], kv_cotangent[0]
    rows = kv_weight.shape[1]
    chips, cores = lax.axis_size(("z", "y", "x")), lax.axis_size("core")
    norm_factor = math.sqrt(inputs_here.shape[0] * chips * cores)
    leaving, staying = product_by_core(inputs_here, cotangent_here, rows)
    leaving, fragment, block_exponent = lax.optimization_barrier(
        (leaving, fragment, block_exponent)
    )
    arrived = lax.ppermute(leaving, "core", [(0, 1), (1, 0)])
    block_scale = jnp.exp2(block_exponent.astype(jnp.float32))[:, None]
    encoded = encode(outer_params, local_params[0], fragment, block_scale)
    partner = lax.ppermute(encoded, "island", [(0, 1), (1, 0), (2, 3), (3, 2)])
    sums, encoded, partner = lax.optimization_barrier(
        (inner_sum(staying, arrived, rows), encoded, partner)
    )
    pieces = lax.all_to_all(sums, ("z", "y", "x"), 0, 0, tiled=True)
    pair = jnp.stack([encoded, partner])
    other_pair = lax.ppermute(pair, "island", [(0, 2), (2, 0), (1, 3), (3, 1)])
    outer_result = outer_step(
        pair, other_pair, outer_params, local_params[0], outer_momentum, fragment, block_scale
    )
    gradient = jnp.sum(pieces.astype(jnp.float32), axis=0) / norm_factor
    inner_result = adamw_step(kv_weight[0], adam_m[0], adam_v[0], gradient)
    return tuple(part[None] for part in inner_result) + outer_result


def solution(mesh):
    grid = Mesh(mesh.devices.reshape(mesh.shape["island"], 3, 8, 4, 2), ("island",) + FSDP)
    in_specs = (
        P("island", FSDP, None),
        P("island", FSDP, None),
        P("island", FSDP, None),
        P("island", FSDP, None),
        P("island", FSDP, None),
        P(None, FSDP),
        P("island", None, FSDP),
        P(None, FSDP),
        P(),
        P(FSDP),
    )
    out_specs = (
        P("island", FSDP, None),
        P("island", FSDP, None),
        P("island", FSDP, None),
        P(None, FSDP),
        P(None, FSDP),
        P("island", None, FSDP),
    )
    return jax.shard_map(
        on_device, mesh=grid, in_specs=in_specs, out_specs=out_specs, check_vma=False
    )
```

```python
import functools
import math

import jax
import jax.numpy as jnp
from jax import lax
from jax.experimental import pallas as pl
from jax.experimental.pallas import tpu as pltpu
from jax.sharding import Mesh
from jax.sharding import PartitionSpec as P

FSDP = ("z", "y", "x", "core")

beta_one = 0.9
beta_two = 0.95
bias_one = 1.0 - 0.9**10
bias_two = 1.0 - 0.95**10
adam_eps = 1e-08
decay_rate = 0.1
inner_rate = 0.01
outer_rate = 0.7
momentum_coef = 0.9
mixing_alpha = 0.5
code_limit = 448.0


def adamw_step(weight, first, second, gradient):
    first_new = beta_one * first + (1.0 - beta_one) * gradient
    second_new = beta_two * second + (1.0 - beta_two) * gradient * gradient
    update = (
        first_new / bias_one / (jnp.sqrt(second_new / bias_two) + adam_eps) + decay_rate * weight
    )
    return (weight - inner_rate * update, first_new, second_new)


def product_kernel(inputs, cotangent, leaving, staying, *, rows):
    product = lax.dot_general(
        inputs[...], cotangent[...], (((0,), (0,)), ((), ())), preferred_element_type=jnp.float32
    )
    product = product.reshape(-1, 2, rows, product.shape[-1])
    first = product[:, 0].reshape(leaving.shape).astype(jnp.bfloat16)
    second = product[:, 1].reshape(leaving.shape).astype(jnp.bfloat16)
    core = lax.axis_index("core")

    @pl.when(core == 0)
    def _():
        staying[...] = first
        leaving[...] = second

    @pl.when(core == 1)
    def _():
        staying[...] = second
        leaving[...] = first


def product_by_core(inputs, cotangent, rows):
    tokens, wide = inputs.shape
    columns = cotangent.shape[1]
    block = wide // 2
    half = jax.ShapeDtypeStruct((wide // 2, columns), jnp.bfloat16)
    out_spec = pl.BlockSpec((block // 2, columns), lambda i: (i, 0))
    return pl.pallas_call(
        functools.partial(product_kernel, rows=rows),
        grid=(wide // block,),
        in_specs=[
            pl.BlockSpec((tokens, block), lambda i: (0, i)),
            pl.BlockSpec((tokens, columns), lambda i: (0, 0)),
        ],
        out_specs=[out_spec, out_spec],
        out_shape=[half, half],
        compiler_params=pltpu.CompilerParams(vmem_limit_bytes=58 * 1024 * 1024),
        cost_estimate=pl.CostEstimate(
            flops=2 * tokens * wide * columns,
            bytes_accessed=2 * (tokens * (wide + columns) + wide * columns),
            transcendentals=0,
        ),
    )(inputs, cotangent)


def piece_along_x(staying, arrived, owner):
    mine, other = (
        lax.dynamic_index_in_dim(half, owner, 1, keepdims=False) for half in (staying, arrived)
    )
    return mine.astype(jnp.float32) + other.astype(jnp.float32)


def nesterov_update(outer_part, moment_part, pseudo):
    moment_new = momentum_coef * moment_part + pseudo
    outer_new = outer_part - outer_rate * (pseudo + momentum_coef * moment_new)
    return (outer_new, moment_new)


def pick(both, fragment, blocks):
    return jnp.where(fragment[0] == 1, both[1], both[0]).reshape(blocks, -1)


def put(both, fragment, new):
    chosen = lax.broadcasted_iota(jnp.int32, both.shape, 0) == fragment[0]
    return jnp.where(chosen, new.reshape(1, -1), both)


def encode(outer_params, local_params, fragment, block_scale):
    blocks = block_scale.shape[0]
    change = pick(outer_params, fragment, blocks) - pick(local_params, fragment, blocks)
    return jnp.clip(change * block_scale, -code_limit, code_limit).astype(jnp.bfloat16)


def outer_step(codes, outer_params, local_params, outer_momentum, fragment, block_scale):
    blocks = block_scale.shape[0]
    mine, one_off, two_off, three_off = (code.astype(jnp.float32) for code in codes)
    summed = (mine + two_off) + (one_off + three_off)
    pseudo = summed / block_scale / len(codes)
    outer_now, moment_now, local_now = (
        pick(both, fragment, blocks) for both in (outer_params, outer_momentum, local_params)
    )
    outer_new, moment_new = nesterov_update(outer_now, moment_now, pseudo)
    merged = mixing_alpha * local_now + (1.0 - mixing_alpha) * outer_new
    return (
        put(outer_params, fragment, outer_new),
        put(outer_momentum, fragment, moment_new),
        put(local_params, fragment, merged)[None],
    )


def on_device(
    normed_input,
    kv_cotangent,
    kv_weight,
    adam_m,
    adam_v,
    outer_params,
    local_params,
    outer_momentum,
    fragment,
    block_exponent,
):
    inputs_here, cotangent_here = normed_input[0], kv_cotangent[0]
    rows = kv_weight.shape[1]
    chips, cores = lax.axis_size(("z", "y", "x")), lax.axis_size("core")
    norm_factor = math.sqrt(inputs_here.shape[0] * chips * cores)
    leaving, staying = product_by_core(inputs_here, cotangent_here, rows)
    arrived = lax.ppermute(leaving, "core", [(0, 1), (1, 0)])
    nx, here = lax.axis_size("x"), lax.axis_index("x")
    staying, arrived = (half.reshape(chips // nx, nx, rows, -1) for half in (staying, arrived))
    pieces = [
        piece_along_x(staying, arrived, lax.rem(here + step, nx)).astype(jnp.bfloat16)
        for step in range(1, nx)
    ]
    pieces, fragment, block_exponent = lax.optimization_barrier((pieces, fragment, block_exponent))
    total = piece_along_x(staying, arrived, here)
    for step, piece in enumerate(pieces, 1):
        piece = lax.ppermute(piece, "x", [(i, (i + step) % nx) for i in range(nx)])
        total = total + piece.astype(jnp.float32)
    block_scale = jnp.exp2(block_exponent.astype(jnp.float32))[:, None]
    encoded = encode(outer_params, local_params[0], fragment, block_scale)
    islands = lax.axis_size("island")
    codes = [encoded] + [
        lax.ppermute(encoded, "island", [(i, (i + step) % islands) for i in range(islands)])
        for step in range(1, islands)
    ]
    total, codes = lax.optimization_barrier((total.astype(jnp.bfloat16), codes))
    gathered = lax.all_to_all(total, ("z", "y"), 0, 0, tiled=True)
    outer_result = outer_step(
        codes, outer_params, local_params[0], outer_momentum, fragment, block_scale
    )
    gradient = jnp.sum(gathered.astype(jnp.float32), axis=0) / norm_factor
    inner_result = adamw_step(kv_weight[0], adam_m[0], adam_v[0], gradient)
    return tuple(part[None] for part in inner_result) + outer_result


def solution(mesh):
    grid = Mesh(mesh.devices.reshape(mesh.shape["island"], 3, 8, 4, 2), ("island",) + FSDP)
    in_specs = (
        P("island", FSDP, None),
        P("island", FSDP, None),
        P("island", FSDP, None),
        P("island", FSDP, None),
        P("island", FSDP, None),
        P(None, FSDP),
        P("island", None, FSDP),
        P(None, FSDP),
        P(),
        P(FSDP),
    )
    out_specs = (
        P("island", FSDP, None),
        P("island", FSDP, None),
        P("island", FSDP, None),
        P(None, FSDP),
        P(None, FSDP),
        P("island", None, FSDP),
    )
    return jax.shard_map(
        on_device, mesh=grid, in_specs=in_specs, out_specs=out_specs, check_vma=False
    )
```

```python
import functools
import math

import jax
import jax.numpy as jnp
from jax import lax
from jax.experimental import pallas as pl
from jax.experimental.pallas import tpu as pltpu
from jax.sharding import Mesh
from jax.sharding import PartitionSpec as P

FSDP = ("z", "y", "x", "core")

beta_one = 0.9
beta_two = 0.95
bias_one = 1.0 - 0.9**10
bias_two = 1.0 - 0.95**10
adam_eps = 1e-08
decay_rate = 0.1
inner_rate = 0.01
outer_rate = 0.7
momentum_coef = 0.9
mixing_alpha = 0.5
code_limit = 448.0


def adamw_step(weight, first, second, gradient):
    first_new = beta_one * first + (1.0 - beta_one) * gradient
    second_new = beta_two * second + (1.0 - beta_two) * gradient * gradient
    update = (
        first_new / bias_one / (jnp.sqrt(second_new / bias_two) + adam_eps) + decay_rate * weight
    )
    return (weight - inner_rate * update, first_new, second_new)


def product_kernel(inputs, cotangent, leaving, staying, x, c, x_sems, c_sem, *, rows, start, block):
    core = lax.axis_index("core")
    arriving = pltpu.make_async_copy(cotangent, c, c_sem)
    arriving.start()
    blocks = [
        pltpu.make_async_copy(
            inputs.at[:, pl.ds(start + at, block)], x.at[:, pl.ds(at, block)], x_sems.at[at // block]
        )
        for at in range(0, x.shape[1], block)
    ]
    for one in blocks:
        one.start()
    arriving.wait()
    for i, one in enumerate(blocks):
        one.wait()
        product = lax.dot_general(
            x[:, i * block : (i + 1) * block],
            c[...],
            (((0,), (0,)), ((), ())),
            preferred_element_type=jnp.float32,
        )
        product = product.reshape(-1, 2, rows, product.shape[-1])
        first = product[:, 0].reshape(block // 2, -1).astype(jnp.bfloat16)
        second = product[:, 1].reshape(block // 2, -1).astype(jnp.bfloat16)
        here = slice(i * block // 2, (i + 1) * block // 2)
        staying[here] = jnp.where(core == 0, first, second)
        leaving[here] = jnp.where(core == 0, second, first)


def product_by_core(inputs, cotangent, rows, start, wide):
    tokens, columns = cotangent.shape
    block = 768
    half = jax.ShapeDtypeStruct((wide // 2, columns), jnp.bfloat16)
    return pl.pallas_call(
        functools.partial(product_kernel, rows=rows, start=start, block=block),
        in_specs=[pl.BlockSpec(memory_space=pl.ANY)] * 2,
        out_specs=[pl.BlockSpec(memory_space=pltpu.VMEM)] * 2,
        out_shape=[half, half],
        scratch_shapes=[
            pltpu.VMEM((tokens, wide), inputs.dtype),
            pltpu.VMEM((tokens, columns), cotangent.dtype),
            pltpu.SemaphoreType.DMA((wide // block,)),
            pltpu.SemaphoreType.DMA,
        ],
        compiler_params=pltpu.CompilerParams(vmem_limit_bytes=44 * 1024 * 1024),
        cost_estimate=pl.CostEstimate(
            flops=2 * tokens * wide * columns,
            bytes_accessed=2 * (tokens * (wide + columns) + wide * columns),
            transcendentals=0,
        ),
    )(inputs, cotangent)


def piece_along_x(staying, arrived, owner):
    mine, other = (
        lax.dynamic_index_in_dim(half, owner, 1, keepdims=False) for half in (staying, arrived)
    )
    return mine.astype(jnp.float32) + other.astype(jnp.float32)


def total_kernel(*refs):
    *parts, total = refs
    each = len(parts) // 2
    for half in range(2):
        mine, *arrived = parts[half * each : (half + 1) * each]
        height = mine.shape[0]
        value = mine[...]
        for piece in arrived:
            value = value + piece[...].astype(jnp.float32)
        total[half * height : (half + 1) * height] = value.astype(total.dtype)


def total_of(parts):
    height, columns = parts[0].shape
    return pl.pallas_call(
        total_kernel,
        in_specs=[pl.BlockSpec(memory_space=pltpu.VMEM)] * len(parts),
        out_specs=pl.BlockSpec(memory_space=pltpu.VMEM),
        out_shape=jax.ShapeDtypeStruct((2 * height, columns), jnp.bfloat16),
        compiler_params=pltpu.CompilerParams(vmem_limit_bytes=16 * 1024 * 1024),
        cost_estimate=pl.CostEstimate(
            flops=len(parts) * height * columns,
            bytes_accessed=4 * len(parts) * height * columns,
            transcendentals=0,
        ),
    )(*parts)


def nesterov_update(outer_part, moment_part, pseudo):
    moment_new = momentum_coef * moment_part + pseudo
    outer_new = outer_part - outer_rate * (pseudo + momentum_coef * moment_new)
    return (outer_new, moment_new)


def pick(both, fragment, blocks):
    return jnp.where(fragment[0] == 1, both[1], both[0]).reshape(blocks, -1)


def put(both, fragment, new):
    chosen = lax.broadcasted_iota(jnp.int32, both.shape, 0) == fragment[0]
    return jnp.where(chosen, new.reshape(1, -1), both)


def encode(outer_params, local_params, fragment, block_scale):
    blocks = block_scale.shape[0]
    change = pick(outer_params, fragment, blocks) - pick(local_params, fragment, blocks)
    return jnp.clip(change * block_scale, -code_limit, code_limit).astype(jnp.bfloat16)


def outer_step(codes, outer_params, local_params, outer_momentum, fragment, block_scale):
    blocks = block_scale.shape[0]
    summed = jnp.sum(codes.astype(jnp.float32), axis=0)
    pseudo = summed / block_scale / codes.shape[0]
    outer_now, moment_now, local_now = (
        pick(both, fragment, blocks) for both in (outer_params, outer_momentum, local_params)
    )
    outer_new, moment_new = nesterov_update(outer_now, moment_now, pseudo)
    merged = mixing_alpha * local_now + (1.0 - mixing_alpha) * outer_new
    return (
        put(outer_params, fragment, outer_new),
        put(outer_momentum, fragment, moment_new),
        put(local_params, fragment, merged)[None],
    )


def on_device(
    normed_input,
    kv_cotangent,
    kv_weight,
    adam_m,
    adam_v,
    outer_params,
    local_params,
    outer_momentum,
    fragment,
    block_exponent,
):
    inputs_here, cotangent_here = normed_input[0], kv_cotangent[0]
    rows = kv_weight.shape[1]
    chips, cores = lax.axis_size(("z", "y", "x")), lax.axis_size("core")
    norm_factor = math.sqrt(inputs_here.shape[0] * chips * cores)
    nx, here = lax.axis_size("x"), lax.axis_index("x")
    half = inputs_here.shape[1] // 2
    parts = []
    for start in (0, half):
        leaving, staying = product_by_core(inputs_here, cotangent_here, rows, start, half)
        arrived = lax.ppermute(leaving, "core", [(0, 1), (1, 0)])
        staying, arrived = (part.reshape(-1, nx, rows, part.shape[1]) for part in (staying, arrived))
        mine = piece_along_x(staying, arrived, here)
        pieces = [
            piece_along_x(staying, arrived, lax.rem(here + step, nx)).astype(jnp.bfloat16)
            for step in range(1, nx)
        ]
        if start:
            pieces, fragment, block_exponent = lax.optimization_barrier(
                (pieces, fragment, block_exponent)
            )
        arrived = [
            lax.ppermute(piece, "x", [(i, (i + step) % nx) for i in range(nx)])
            for step, piece in enumerate(pieces, 1)
        ]
        parts += [part.reshape(-1, part.shape[-1]) for part in [mine] + arrived]
    block_scale = jnp.exp2(block_exponent.astype(jnp.float32))[:, None]
    encoded = encode(outer_params, local_params[0], fragment, block_scale)
    copies = jnp.broadcast_to(encoded, (lax.axis_size("island"),) + encoded.shape)
    codes = lax.all_to_all(copies, "island", 0, 0, tiled=True)
    total, codes = lax.optimization_barrier((total_of(parts), codes))
    gathered = lax.all_to_all(
        total.reshape(chips // nx, rows, -1), ("z", "y"), 0, 0, tiled=True
    )
    outer_result = outer_step(
        codes, outer_params, local_params[0], outer_momentum, fragment, block_scale
    )
    gradient = jnp.sum(gathered.astype(jnp.float32), axis=0) / norm_factor
    inner_result = adamw_step(kv_weight[0], adam_m[0], adam_v[0], gradient)
    return tuple(part[None] for part in inner_result) + outer_result


def solution(mesh):
    grid = Mesh(mesh.devices.reshape(mesh.shape["island"], 3, 8, 4, 2), ("island",) + FSDP)
    in_specs = (
        P("island", FSDP, None),
        P("island", FSDP, None),
        P("island", FSDP, None),
        P("island", FSDP, None),
        P("island", FSDP, None),
        P(None, FSDP),
        P("island", None, FSDP),
        P(None, FSDP),
        P(),
        P(FSDP),
    )
    out_specs = (
        P("island", FSDP, None),
        P("island", FSDP, None),
        P("island", FSDP, None),
        P(None, FSDP),
        P(None, FSDP),
        P("island", None, FSDP),
    )
    return jax.shard_map(
        on_device, mesh=grid, in_specs=in_specs, out_specs=out_specs, check_vma=False
    )
```

```python
import functools
import math

import jax
import jax.numpy as jnp
from jax import lax
from jax.experimental import pallas as pl
from jax.experimental.pallas import tpu as pltpu
from jax.sharding import Mesh
from jax.sharding import PartitionSpec as P

FSDP = ("z", "y", "x", "core")

beta_one = 0.9
beta_two = 0.95
bias_one = 1.0 - 0.9**10
bias_two = 1.0 - 0.95**10
adam_eps = 1e-08
decay_rate = 0.1
inner_rate = 0.01
outer_rate = 0.7
momentum_coef = 0.9
mixing_alpha = 0.5
code_limit = 448.0


def adamw_step(weight, first, second, gradient):
    first_new = beta_one * first + (1.0 - beta_one) * gradient
    second_new = beta_two * second + (1.0 - beta_two) * gradient * gradient
    update = (
        first_new / bias_one / (jnp.sqrt(second_new / bias_two) + adam_eps) + decay_rate * weight
    )
    return (weight - inner_rate * update, first_new, second_new)


def product_kernel(inputs, cotangent, leaving, staying, *, rows):
    product = lax.dot_general(
        inputs[...], cotangent[...], (((0,), (0,)), ((), ())), preferred_element_type=jnp.float32
    )
    product = product.reshape(-1, 2, rows, product.shape[-1])
    first = product[:, 0].reshape(leaving.shape).astype(jnp.bfloat16)
    second = product[:, 1].reshape(leaving.shape).astype(jnp.bfloat16)
    core = lax.axis_index("core")

    @pl.when(core == 0)
    def _():
        staying[...] = first
        leaving[...] = second

    @pl.when(core == 1)
    def _():
        staying[...] = second
        leaving[...] = first


def product_by_core(inputs, cotangent, rows):
    tokens, wide = inputs.shape
    columns = cotangent.shape[1]
    block = wide // 2
    half = jax.ShapeDtypeStruct((wide // 2, columns), jnp.bfloat16)
    out_spec = pl.BlockSpec((block // 2, columns), lambda i: (i, 0))
    return pl.pallas_call(
        functools.partial(product_kernel, rows=rows),
        grid=(wide // block,),
        in_specs=[
            pl.BlockSpec((tokens, block), lambda i: (0, i)),
            pl.BlockSpec((tokens, columns), lambda i: (0, 0)),
        ],
        out_specs=[out_spec, out_spec],
        out_shape=[half, half],
        compiler_params=pltpu.CompilerParams(vmem_limit_bytes=58 * 1024 * 1024),
        cost_estimate=pl.CostEstimate(
            flops=2 * tokens * wide * columns,
            bytes_accessed=2 * (tokens * (wide + columns) + wide * columns),
            transcendentals=0,
        ),
    )(inputs, cotangent)


def piece_along_x(staying, arrived, owner):
    mine, other = (
        lax.dynamic_index_in_dim(half, owner, 1, keepdims=False) for half in (staying, arrived)
    )
    return mine.astype(jnp.float32) + other.astype(jnp.float32)


def total_kernel(mine, *refs):
    *arrived, total = refs
    value = mine[...]
    for piece in arrived:
        value = value + piece[...].astype(jnp.float32)
    total[...] = value.astype(total.dtype)


def total_of(mine, arrived):
    return pl.pallas_call(
        total_kernel,
        in_specs=[pl.BlockSpec(memory_space=pltpu.VMEM)] * (1 + len(arrived)),
        out_specs=pl.BlockSpec(memory_space=pltpu.VMEM),
        out_shape=jax.ShapeDtypeStruct(mine.shape, jnp.bfloat16),
        compiler_params=pltpu.CompilerParams(vmem_limit_bytes=16 * 1024 * 1024),
        cost_estimate=pl.CostEstimate(
            flops=4 * mine.size, bytes_accessed=12 * mine.size, transcendentals=0
        ),
    )(mine, *arrived)


def later_kernel(value, before, same):
    del before
    same[...] = value[...]


def later(value, before):
    return pl.pallas_call(
        later_kernel,
        in_specs=[pl.BlockSpec(memory_space=pltpu.VMEM), pl.BlockSpec(memory_space=pl.ANY)],
        out_specs=pl.BlockSpec(memory_space=pltpu.VMEM),
        out_shape=jax.ShapeDtypeStruct(value.shape, value.dtype),
        compiler_params=pltpu.CompilerParams(vmem_limit_bytes=8 * 1024 * 1024),
    )(value, before)


def owner_kernel(before, owner, *, step):
    del before
    owner[0] = lax.rem(lax.axis_index("x") + step, lax.axis_size("x"))


def owner_later(step, before):
    return pl.pallas_call(
        functools.partial(owner_kernel, step=step),
        in_specs=[pl.BlockSpec(memory_space=pl.ANY)],
        out_specs=pl.BlockSpec(memory_space=pltpu.SMEM),
        out_shape=jax.ShapeDtypeStruct((1,), jnp.int32),
        compiler_params=pltpu.CompilerParams(vmem_limit_bytes=8 * 1024 * 1024),
    )(before)[0]


def along_zy(pieces):
    arrived = lax.all_to_all(pieces, ("z", "y"), 0, 0, tiled=True)
    return jnp.sum(arrived.astype(jnp.float32), axis=0)


def along_ring(value, axis, step):
    size = lax.axis_size(axis)
    return lax.ppermute(value, axis, [(i, (i + step) % size) for i in range(size)])


def nesterov_update(outer_part, moment_part, pseudo):
    moment_new = momentum_coef * moment_part + pseudo
    outer_new = outer_part - outer_rate * (pseudo + momentum_coef * moment_new)
    return (outer_new, moment_new)


def pick(both, fragment, blocks):
    return jnp.where(fragment[0] == 1, both[1], both[0]).reshape(blocks, -1)


def put(both, fragment, new):
    chosen = lax.broadcasted_iota(jnp.int32, both.shape, 0) == fragment[0]
    return jnp.where(chosen, new.reshape(1, -1), both)


def encode(outer_params, local_params, fragment, block_scale):
    blocks = block_scale.shape[0]
    change = pick(outer_params, fragment, blocks) - pick(local_params, fragment, blocks)
    return jnp.clip(change * block_scale, -code_limit, code_limit).astype(jnp.bfloat16)


def outer_step(codes, outer_params, local_params, outer_momentum, fragment, block_scale):
    blocks = block_scale.shape[0]
    codes = [code.astype(jnp.float32) for code in codes]
    summed = (codes[0] + codes[2]) + (codes[1] + codes[3])
    pseudo = summed / block_scale / len(codes)
    outer_now, moment_now, local_now = (
        pick(both, fragment, blocks) for both in (outer_params, outer_momentum, local_params)
    )
    outer_new, moment_new = nesterov_update(outer_now, moment_now, pseudo)
    merged = mixing_alpha * local_now + (1.0 - mixing_alpha) * outer_new
    return (
        put(outer_params, fragment, outer_new),
        put(outer_momentum, fragment, moment_new),
        put(local_params, fragment, merged)[None],
    )


def on_device(
    normed_input,
    kv_cotangent,
    kv_weight,
    adam_m,
    adam_v,
    outer_params,
    local_params,
    outer_momentum,
    fragment,
    block_exponent,
):
    inputs_here, cotangent_here = normed_input[0], kv_cotangent[0]
    rows = kv_weight.shape[1]
    chips, cores = lax.axis_size(("z", "y", "x")), lax.axis_size("core")
    norm_factor = math.sqrt(inputs_here.shape[0] * chips * cores)
    nx, here = lax.axis_size("x"), lax.axis_index("x")
    leaving, staying = product_by_core(inputs_here, cotangent_here, rows)
    arrived = lax.ppermute(leaving, "core", [(0, 1), (1, 0)])
    staying, arrived = (half.reshape(chips // nx, nx, rows, -1) for half in (staying, arrived))
    mine, right, left = (
        piece_along_x(staying, arrived, lax.rem(here + step, nx)) for step in (0, 1, nx - 1)
    )
    right, left = right.astype(jnp.bfloat16), left.astype(jnp.bfloat16)
    far = piece_along_x(staying, arrived, owner_later(2, left)).astype(jnp.bfloat16)
    far = along_zy(far).astype(jnp.bfloat16)
    near = [
        along_ring(piece, "x", step).reshape(-1, mine.shape[-1])
        for piece, step in ((right, 1), (left, nx - 1))
    ]
    total = total_of(mine.reshape(-1, mine.shape[-1]), near)
    summed = along_zy(total.reshape(mine.shape)) + along_ring(far, "x", 2).astype(jnp.float32)
    block_scale = jnp.exp2(block_exponent.astype(jnp.float32))[:, None]
    encoded = later(encode(outer_params, local_params[0], fragment, block_scale), total)
    codes = [encoded] + [
        along_ring(encoded, "island", step) for step in range(1, lax.axis_size("island"))
    ]
    codes[0] = later(encoded, far)
    outer_result = outer_step(
        codes, outer_params, local_params[0], outer_momentum, fragment, block_scale
    )
    inner_result = adamw_step(kv_weight[0], adam_m[0], adam_v[0], summed / norm_factor)
    return tuple(part[None] for part in inner_result) + outer_result


def solution(mesh):
    grid = Mesh(mesh.devices.reshape(mesh.shape["island"], 3, 8, 4, 2), ("island",) + FSDP)
    in_specs = (
        P("island", FSDP, None),
        P("island", FSDP, None),
        P("island", FSDP, None),
        P("island", FSDP, None),
        P("island", FSDP, None),
        P(None, FSDP),
        P("island", None, FSDP),
        P(None, FSDP),
        P(),
        P(FSDP),
    )
    out_specs = (
        P("island", FSDP, None),
        P("island", FSDP, None),
        P("island", FSDP, None),
        P(None, FSDP),
        P(None, FSDP),
        P("island", None, FSDP),
    )
    return jax.shard_map(
        on_device, mesh=grid, in_specs=in_specs, out_specs=out_specs, check_vma=False
    )
```

```python
import functools
import math

import jax
import jax.numpy as jnp
from jax import lax
from jax.experimental import pallas as pl
from jax.experimental.pallas import tpu as pltpu
from jax.sharding import Mesh
from jax.sharding import PartitionSpec as P

FSDP = ("z", "y", "x", "core")

beta_one = 0.9
beta_two = 0.95
bias_one = 1.0 - 0.9**10
bias_two = 1.0 - 0.95**10
adam_eps = 1e-08
decay_rate = 0.1
inner_rate = 0.01
outer_rate = 0.7
momentum_coef = 0.9
mixing_alpha = 0.5
code_limit = 448.0


def adamw_step(weight, first, second, gradient):
    first_new = beta_one * first + (1.0 - beta_one) * gradient
    second_new = beta_two * second + (1.0 - beta_two) * gradient * gradient
    update = (
        first_new / bias_one / (jnp.sqrt(second_new / bias_two) + adam_eps) + decay_rate * weight
    )
    return (weight - inner_rate * update, first_new, second_new)


def product_kernel(inputs, cotangent, leaving, staying, *, rows):
    product = lax.dot_general(
        inputs[...], cotangent[...], (((0,), (0,)), ((), ())), preferred_element_type=jnp.float32
    )
    product = product.reshape(-1, 2, rows, product.shape[-1])
    first = product[:, 0].reshape(leaving.shape).astype(jnp.bfloat16)
    second = product[:, 1].reshape(leaving.shape).astype(jnp.bfloat16)
    core = lax.axis_index("core")

    @pl.when(core == 0)
    def _():
        staying[...] = first
        leaving[...] = second

    @pl.when(core == 1)
    def _():
        staying[...] = second
        leaving[...] = first


def product_by_core(inputs, cotangent, rows):
    tokens, wide = inputs.shape
    columns = cotangent.shape[1]
    block = wide // 2
    half = jax.ShapeDtypeStruct((wide // 2, columns), jnp.bfloat16)
    out_spec = pl.BlockSpec((block // 2, columns), lambda i: (i, 0))
    return pl.pallas_call(
        functools.partial(product_kernel, rows=rows),
        grid=(wide // block,),
        in_specs=[
            pl.BlockSpec((tokens, block), lambda i: (0, i)),
            pl.BlockSpec((tokens, columns), lambda i: (0, 0)),
        ],
        out_specs=[out_spec, out_spec],
        out_shape=[half, half],
        compiler_params=pltpu.CompilerParams(vmem_limit_bytes=58 * 1024 * 1024),
        cost_estimate=pl.CostEstimate(
            flops=2 * tokens * wide * columns,
            bytes_accessed=2 * (tokens * (wide + columns) + wide * columns),
            transcendentals=0,
        ),
    )(inputs, cotangent)


def piece_along_x(staying, arrived, owner):
    mine, other = (
        lax.dynamic_index_in_dim(half, owner, 1, keepdims=False) for half in (staying, arrived)
    )
    return mine.astype(jnp.float32) + other.astype(jnp.float32)


def total_kernel(mine, *refs):
    *arrived, total = refs
    value = mine[...]
    for piece in arrived:
        value = value + piece[...].astype(jnp.float32)
    total[...] = value.astype(total.dtype)


def total_of(mine, arrived):
    return pl.pallas_call(
        total_kernel,
        in_specs=[pl.BlockSpec(memory_space=pltpu.VMEM)] * (1 + len(arrived)),
        out_specs=pl.BlockSpec(memory_space=pltpu.VMEM),
        out_shape=jax.ShapeDtypeStruct(mine.shape, jnp.bfloat16),
        compiler_params=pltpu.CompilerParams(vmem_limit_bytes=16 * 1024 * 1024),
        cost_estimate=pl.CostEstimate(
            flops=4 * mine.size, bytes_accessed=12 * mine.size, transcendentals=0
        ),
    )(mine, *arrived)


def copies_kernel(encoded, before, copies):
    del before
    for i in range(copies.shape[0]):
        copies[i] = encoded[...]


def copies_of(encoded, count, before):
    return pl.pallas_call(
        copies_kernel,
        in_specs=[pl.BlockSpec(memory_space=pltpu.VMEM), pl.BlockSpec(memory_space=pl.ANY)],
        out_specs=pl.BlockSpec(memory_space=pltpu.VMEM),
        out_shape=jax.ShapeDtypeStruct((count,) + encoded.shape, encoded.dtype),
        compiler_params=pltpu.CompilerParams(vmem_limit_bytes=8 * 1024 * 1024),
    )(encoded, before)


def nesterov_update(outer_part, moment_part, pseudo):
    moment_new = momentum_coef * moment_part + pseudo
    outer_new = outer_part - outer_rate * (pseudo + momentum_coef * moment_new)
    return (outer_new, moment_new)


def pick(both, fragment, blocks):
    return jnp.where(fragment[0] == 1, both[1], both[0]).reshape(blocks, -1)


def put(both, fragment, new):
    chosen = lax.broadcasted_iota(jnp.int32, both.shape, 0) == fragment[0]
    return jnp.where(chosen, new.reshape(1, -1), both)


def encode(outer_params, local_params, fragment, block_scale):
    blocks = block_scale.shape[0]
    change = pick(outer_params, fragment, blocks) - pick(local_params, fragment, blocks)
    return jnp.clip(change * block_scale, -code_limit, code_limit).astype(jnp.bfloat16)


def outer_step(codes, outer_params, local_params, outer_momentum, fragment, block_scale):
    blocks = block_scale.shape[0]
    summed = jnp.sum(codes.astype(jnp.float32), axis=0)
    pseudo = summed / block_scale / codes.shape[0]
    outer_now, moment_now, local_now = (
        pick(both, fragment, blocks) for both in (outer_params, outer_momentum, local_params)
    )
    outer_new, moment_new = nesterov_update(outer_now, moment_now, pseudo)
    merged = mixing_alpha * local_now + (1.0 - mixing_alpha) * outer_new
    return (
        put(outer_params, fragment, outer_new),
        put(outer_momentum, fragment, moment_new),
        put(local_params, fragment, merged)[None],
    )


def on_device(
    normed_input,
    kv_cotangent,
    kv_weight,
    adam_m,
    adam_v,
    outer_params,
    local_params,
    outer_momentum,
    fragment,
    block_exponent,
):
    inputs_here, cotangent_here = normed_input[0], kv_cotangent[0]
    rows = kv_weight.shape[1]
    chips, cores = lax.axis_size(("z", "y", "x")), lax.axis_size("core")
    norm_factor = math.sqrt(inputs_here.shape[0] * chips * cores)
    nx, here = lax.axis_size("x"), lax.axis_index("x")
    block_scale = jnp.exp2(block_exponent.astype(jnp.float32))[:, None]
    encoded = encode(outer_params, local_params[0], fragment, block_scale)
    leaving, staying = product_by_core(inputs_here, cotangent_here, rows)
    arrived = lax.ppermute(leaving, "core", [(0, 1), (1, 0)])
    staying, arrived = (half.reshape(chips // nx, nx, rows, -1) for half in (staying, arrived))
    pieces = [
        piece_along_x(staying, arrived, lax.rem(here + step, nx)).astype(jnp.bfloat16)
        for step in range(1, nx)
    ]
    mine = piece_along_x(staying, arrived, here)
    copies = copies_of(encoded, lax.axis_size("island"), pieces[-1])
    codes = lax.all_to_all(copies, "island", 0, 0, tiled=True)
    pieces = [
        lax.ppermute(piece, "x", [(i, (i + step) % nx) for i in range(nx)])
        for step, piece in enumerate(pieces, 1)
    ]
    mine, *pieces = (part.reshape(-1, part.shape[-1]) for part in [mine] + pieces)
    total, codes = lax.optimization_barrier((total_of(mine, pieces), codes))
    gathered = lax.all_to_all(
        total.reshape(chips // nx, rows, -1), ("z", "y"), 0, 0, tiled=True
    )
    outer_result = outer_step(
        codes, outer_params, local_params[0], outer_momentum, fragment, block_scale
    )
    gradient = jnp.sum(gathered.astype(jnp.float32), axis=0) / norm_factor
    inner_result = adamw_step(kv_weight[0], adam_m[0], adam_v[0], gradient)
    return tuple(part[None] for part in inner_result) + outer_result


def solution(mesh):
    grid = Mesh(mesh.devices.reshape(mesh.shape["island"], 3, 8, 4, 2), ("island",) + FSDP)
    in_specs = (
        P("island", FSDP, None),
        P("island", FSDP, None),
        P("island", FSDP, None),
        P("island", FSDP, None),
        P("island", FSDP, None),
        P(None, FSDP),
        P("island", None, FSDP),
        P(None, FSDP),
        P(),
        P(FSDP),
    )
    out_specs = (
        P("island", FSDP, None),
        P("island", FSDP, None),
        P("island", FSDP, None),
        P(None, FSDP),
        P(None, FSDP),
        P("island", None, FSDP),
    )
    return jax.shard_map(
        on_device, mesh=grid, in_specs=in_specs, out_specs=out_specs, check_vma=False
    )
```

```python
import functools
import math

import jax
import jax.numpy as jnp
from jax import lax
from jax.experimental import pallas as pl
from jax.experimental.pallas import tpu as pltpu
from jax.sharding import Mesh
from jax.sharding import PartitionSpec as P

FSDP = ("z", "y", "x", "core")

beta_one = 0.9
beta_two = 0.95
bias_one = 1.0 - 0.9**10
bias_two = 1.0 - 0.95**10
adam_eps = 1e-08
decay_rate = 0.1
inner_rate = 0.01
outer_rate = 0.7
momentum_coef = 0.9
mixing_alpha = 0.5
code_limit = 448.0


def adamw_step(weight, first, second, gradient):
    first_new = beta_one * first + (1.0 - beta_one) * gradient
    second_new = beta_two * second + (1.0 - beta_two) * gradient * gradient
    update = (
        first_new / bias_one / (jnp.sqrt(second_new / bias_two) + adam_eps) + decay_rate * weight
    )
    return (weight - inner_rate * update, first_new, second_new)


def product_kernel(inputs, cotangent, leaving, staying, *, rows):
    product = lax.dot_general(
        inputs[...], cotangent[...], (((0,), (0,)), ((), ())), preferred_element_type=jnp.float32
    )
    product = product.reshape(-1, 2, rows, product.shape[-1])
    first = product[:, 0].reshape(leaving.shape).astype(jnp.bfloat16)
    second = product[:, 1].reshape(leaving.shape).astype(jnp.bfloat16)
    core = lax.axis_index("core")

    @pl.when(core == 0)
    def _():
        staying[...] = first
        leaving[...] = second

    @pl.when(core == 1)
    def _():
        staying[...] = second
        leaving[...] = first


def product_by_core(inputs, cotangent, rows):
    tokens, wide = inputs.shape
    columns = cotangent.shape[1]
    block = wide // 2
    half = jax.ShapeDtypeStruct((wide // 2, columns), jnp.bfloat16)
    out_spec = pl.BlockSpec((block // 2, columns), lambda i: (i, 0))
    return pl.pallas_call(
        functools.partial(product_kernel, rows=rows),
        grid=(wide // block,),
        in_specs=[
            pl.BlockSpec((tokens, block), lambda i: (0, i)),
            pl.BlockSpec((tokens, columns), lambda i: (0, 0)),
        ],
        out_specs=[out_spec, out_spec],
        out_shape=[half, half],
        compiler_params=pltpu.CompilerParams(vmem_limit_bytes=58 * 1024 * 1024),
        cost_estimate=pl.CostEstimate(
            flops=2 * tokens * wide * columns,
            bytes_accessed=2 * (tokens * (wide + columns) + wide * columns),
            transcendentals=0,
        ),
    )(inputs, cotangent)


def pack_kernel(staying, arrived, packed):
    owners, height, columns = packed.shape
    value = staying[...].astype(jnp.float32) + arrived[...].astype(jnp.float32)
    value = value.reshape(-1, owners, 24, columns)
    for owner in range(owners):
        packed[owner] = value[:, owner].reshape(height, columns).astype(packed.dtype)


def packed_by_owner(staying, arrived, owners):
    height, columns = staying.shape
    steps = 4
    in_spec = pl.BlockSpec((height // steps, columns), lambda i: (i, 0))
    return pl.pallas_call(
        pack_kernel,
        grid=(steps,),
        in_specs=[in_spec, in_spec],
        out_specs=pl.BlockSpec((owners, height // owners // steps, columns), lambda i: (0, i, 0)),
        out_shape=jax.ShapeDtypeStruct((owners, height // owners, columns), staying.dtype),
        compiler_params=pltpu.CompilerParams(vmem_limit_bytes=32 * 1024 * 1024),
        cost_estimate=pl.CostEstimate(
            flops=height * columns, bytes_accessed=6 * height * columns, transcendentals=0
        ),
    )(staying, arrived)


def total_kernel(pieces, total):
    value = pieces[0].astype(jnp.float32)
    for source in range(1, pieces.shape[0]):
        value = value + pieces[source].astype(jnp.float32)
    total[...] = value.astype(total.dtype)


def total_of(pieces):
    count, height, columns = pieces.shape
    return pl.pallas_call(
        total_kernel,
        in_specs=[pl.BlockSpec(memory_space=pltpu.VMEM)],
        out_specs=pl.BlockSpec(memory_space=pltpu.VMEM),
        out_shape=jax.ShapeDtypeStruct((height, columns), jnp.bfloat16),
        compiler_params=pltpu.CompilerParams(vmem_limit_bytes=16 * 1024 * 1024),
        cost_estimate=pl.CostEstimate(
            flops=count * height * columns,
            bytes_accessed=2 * (count + 1) * height * columns,
            transcendentals=0,
        ),
    )(pieces)


def later_kernel(value, before, same):
    del before
    same[...] = value[...]


def later(value, before):
    return pl.pallas_call(
        later_kernel,
        in_specs=[pl.BlockSpec(memory_space=pltpu.VMEM), pl.BlockSpec(memory_space=pl.ANY)],
        out_specs=pl.BlockSpec(memory_space=pltpu.VMEM),
        out_shape=jax.ShapeDtypeStruct(value.shape, value.dtype),
        compiler_params=pltpu.CompilerParams(vmem_limit_bytes=8 * 1024 * 1024),
    )(value, before)


def nesterov_update(outer_part, moment_part, pseudo):
    moment_new = momentum_coef * moment_part + pseudo
    outer_new = outer_part - outer_rate * (pseudo + momentum_coef * moment_new)
    return (outer_new, moment_new)


def pick(both, fragment, blocks):
    return jnp.where(fragment[0] == 1, both[1], both[0]).reshape(blocks, -1)


def put(both, fragment, new):
    chosen = lax.broadcasted_iota(jnp.int32, both.shape, 0) == fragment[0]
    return jnp.where(chosen, new.reshape(1, -1), both)


def encode(outer_params, local_params, fragment, block_scale):
    blocks = block_scale.shape[0]
    change = pick(outer_params, fragment, blocks) - pick(local_params, fragment, blocks)
    return jnp.clip(change * block_scale, -code_limit, code_limit).astype(jnp.bfloat16)


def outer_step(codes, outer_params, local_params, outer_momentum, fragment, block_scale):
    blocks = block_scale.shape[0]
    codes = [code.astype(jnp.float32) for code in codes]
    summed = (codes[0] + codes[2]) + (codes[1] + codes[3])
    pseudo = summed / block_scale / len(codes)
    outer_now, moment_now, local_now = (
        pick(both, fragment, blocks) for both in (outer_params, outer_momentum, local_params)
    )
    outer_new, moment_new = nesterov_update(outer_now, moment_now, pseudo)
    merged = mixing_alpha * local_now + (1.0 - mixing_alpha) * outer_new
    return (
        put(outer_params, fragment, outer_new),
        put(outer_momentum, fragment, moment_new),
        put(local_params, fragment, merged)[None],
    )


def on_device(
    normed_input,
    kv_cotangent,
    kv_weight,
    adam_m,
    adam_v,
    outer_params,
    local_params,
    outer_momentum,
    fragment,
    block_exponent,
):
    inputs_here, cotangent_here = normed_input[0], kv_cotangent[0]
    rows = kv_weight.shape[1]
    chips, cores = lax.axis_size(("z", "y", "x")), lax.axis_size("core")
    norm_factor = math.sqrt(inputs_here.shape[0] * chips * cores)
    nx = lax.axis_size("x")
    block_scale = jnp.exp2(block_exponent.astype(jnp.float32))[:, None]
    encoded = encode(outer_params, local_params[0], fragment, block_scale)
    leaving, staying = product_by_core(inputs_here, cotangent_here, rows)
    arrived = lax.ppermute(leaving, "core", [(0, 1), (1, 0)])
    packed = packed_by_owner(staying, arrived, nx)
    pieces = lax.all_to_all(packed, "x", 0, 0, tiled=True)
    encoded = later(encoded, packed)
    islands = lax.axis_size("island")
    codes = [encoded] + [
        lax.ppermute(encoded, "island", [(i, (i + step) % islands) for i in range(islands)])
        for step in range(1, islands)
    ]
    total, codes = lax.optimization_barrier((total_of(pieces), codes))
    gathered = lax.all_to_all(
        total.reshape(chips // nx, rows, -1), ("z", "y"), 0, 0, tiled=True
    )
    outer_result = outer_step(
        codes, outer_params, local_params[0], outer_momentum, fragment, block_scale
    )
    gradient = jnp.sum(gathered.astype(jnp.float32), axis=0) / norm_factor
    inner_result = adamw_step(kv_weight[0], adam_m[0], adam_v[0], gradient)
    return tuple(part[None] for part in inner_result) + outer_result


def solution(mesh):
    grid = Mesh(mesh.devices.reshape(mesh.shape["island"], 3, 8, 4, 2), ("island",) + FSDP)
    in_specs = (
        P("island", FSDP, None),
        P("island", FSDP, None),
        P("island", FSDP, None),
        P("island", FSDP, None),
        P("island", FSDP, None),
        P(None, FSDP),
        P("island", None, FSDP),
        P(None, FSDP),
        P(),
        P(FSDP),
    )
    out_specs = (
        P("island", FSDP, None),
        P("island", FSDP, None),
        P("island", FSDP, None),
        P(None, FSDP),
        P(None, FSDP),
        P("island", None, FSDP),
    )
    return jax.shard_map(
        on_device, mesh=grid, in_specs=in_specs, out_specs=out_specs, check_vma=False
    )
```

```python
import functools
import math

import jax
import jax.numpy as jnp
from jax import lax
from jax.experimental import pallas as pl
from jax.experimental.pallas import tpu as pltpu
from jax.sharding import Mesh
from jax.sharding import PartitionSpec as P

FSDP = ("z", "y", "x", "core")

beta_one = 0.9
beta_two = 0.95
bias_one = 1.0 - 0.9**10
bias_two = 1.0 - 0.95**10
adam_eps = 1e-08
decay_rate = 0.1
inner_rate = 0.01
outer_rate = 0.7
momentum_coef = 0.9
mixing_alpha = 0.5
code_limit = 448.0


def adamw_step(weight, first, second, gradient):
    first_new = beta_one * first + (1.0 - beta_one) * gradient
    second_new = beta_two * second + (1.0 - beta_two) * gradient * gradient
    update = (
        first_new / bias_one / (jnp.sqrt(second_new / bias_two) + adam_eps) + decay_rate * weight
    )
    return (weight - inner_rate * update, first_new, second_new)


def product_kernel(inputs, cotangent, leaving, staying, *, rows):
    product = lax.dot_general(
        inputs[...], cotangent[...], (((0,), (0,)), ((), ())), preferred_element_type=jnp.float32
    )
    product = product.reshape(-1, 2, rows, product.shape[-1])
    first = product[:, 0].reshape(leaving.shape).astype(jnp.bfloat16)
    second = product[:, 1].reshape(leaving.shape).astype(jnp.bfloat16)
    core = lax.axis_index("core")

    @pl.when(core == 0)
    def _():
        staying[...] = first
        leaving[...] = second

    @pl.when(core == 1)
    def _():
        staying[...] = second
        leaving[...] = first


def product_by_core(inputs, cotangent, rows):
    tokens, wide = inputs.shape
    columns = cotangent.shape[1]
    block = wide // 2
    half = jax.ShapeDtypeStruct((wide // 2, columns), jnp.bfloat16)
    out_spec = pl.BlockSpec((block // 2, columns), lambda i: (i, 0))
    return pl.pallas_call(
        functools.partial(product_kernel, rows=rows),
        grid=(wide // block,),
        in_specs=[
            pl.BlockSpec((tokens, block), lambda i: (0, i)),
            pl.BlockSpec((tokens, columns), lambda i: (0, 0)),
        ],
        out_specs=[out_spec, out_spec],
        out_shape=[half, half],
        compiler_params=pltpu.CompilerParams(vmem_limit_bytes=58 * 1024 * 1024),
        cost_estimate=pl.CostEstimate(
            flops=2 * tokens * wide * columns,
            bytes_accessed=2 * (tokens * (wide + columns) + wide * columns),
            transcendentals=0,
        ),
    )(inputs, cotangent)


def fetch_kernel(there, here, sem):
    copy = pltpu.make_async_copy(there, here, sem)
    copy.start()
    copy.wait()


def fetched(value):
    return pl.pallas_call(
        fetch_kernel,
        in_specs=[pl.BlockSpec(memory_space=pl.ANY)],
        out_specs=pl.BlockSpec(memory_space=pltpu.VMEM),
        out_shape=jax.ShapeDtypeStruct(value.shape, value.dtype),
        scratch_shapes=[pltpu.SemaphoreType.DMA],
        compiler_params=pltpu.CompilerParams(vmem_limit_bytes=8 * 1024 * 1024),
    )(value)


def pack_kernel(staying, arrived, packed):
    owners, height, columns = packed.shape
    value = staying[...].astype(jnp.float32) + arrived[...].astype(jnp.float32)
    value = value.reshape(-1, owners, 24, columns)
    for owner in range(owners):
        packed[owner] = value[:, owner].reshape(height, columns).astype(packed.dtype)


def packed_by_owner(staying, arrived, owners):
    height, columns = staying.shape
    steps = 4
    in_spec = pl.BlockSpec((height // steps, columns), lambda i: (i, 0))
    return pl.pallas_call(
        pack_kernel,
        grid=(steps,),
        in_specs=[in_spec, in_spec],
        out_specs=pl.BlockSpec((owners, height // owners // steps, columns), lambda i: (0, i, 0)),
        out_shape=jax.ShapeDtypeStruct((owners, height // owners, columns), staying.dtype),
        compiler_params=pltpu.CompilerParams(vmem_limit_bytes=32 * 1024 * 1024),
        cost_estimate=pl.CostEstimate(
            flops=height * columns, bytes_accessed=6 * height * columns, transcendentals=0
        ),
    )(staying, arrived)


def total_kernel(pieces, total):
    value = pieces[0].astype(jnp.float32)
    for source in range(1, pieces.shape[0]):
        value = value + pieces[source].astype(jnp.float32)
    total[...] = value.astype(total.dtype)


def total_of(pieces):
    count, height, columns = pieces.shape
    return pl.pallas_call(
        total_kernel,
        in_specs=[pl.BlockSpec(memory_space=pltpu.VMEM)],
        out_specs=pl.BlockSpec(memory_space=pltpu.VMEM),
        out_shape=jax.ShapeDtypeStruct((height, columns), jnp.bfloat16),
        compiler_params=pltpu.CompilerParams(vmem_limit_bytes=16 * 1024 * 1024),
        cost_estimate=pl.CostEstimate(
            flops=count * height * columns,
            bytes_accessed=2 * (count + 1) * height * columns,
            transcendentals=0,
        ),
    )(pieces)


def later_kernel(value, before, same):
    del before
    same[...] = value[...]


def later(value, before):
    return pl.pallas_call(
        later_kernel,
        in_specs=[pl.BlockSpec(memory_space=pltpu.VMEM), pl.BlockSpec(memory_space=pl.ANY)],
        out_specs=pl.BlockSpec(memory_space=pltpu.VMEM),
        out_shape=jax.ShapeDtypeStruct(value.shape, value.dtype),
        compiler_params=pltpu.CompilerParams(vmem_limit_bytes=8 * 1024 * 1024),
    )(value, before)


def nesterov_update(outer_part, moment_part, pseudo):
    moment_new = momentum_coef * moment_part + pseudo
    outer_new = outer_part - outer_rate * (pseudo + momentum_coef * moment_new)
    return (outer_new, moment_new)


def pick(both, fragment, blocks):
    return jnp.where(fragment[0] == 1, both[1], both[0]).reshape(blocks, -1)


def put(both, fragment, new):
    chosen = lax.broadcasted_iota(jnp.int32, both.shape, 0) == fragment[0]
    return jnp.where(chosen, new.reshape(1, -1), both)


def encode(outer_params, local_params, fragment, block_scale):
    blocks = block_scale.shape[0]
    change = pick(outer_params, fragment, blocks) - pick(local_params, fragment, blocks)
    return jnp.clip(change * block_scale, -code_limit, code_limit).astype(jnp.bfloat16)


def outer_step(codes, outer_params, local_params, outer_momentum, fragment, block_scale):
    blocks = block_scale.shape[0]
    codes = [code.astype(jnp.float32) for code in codes]
    summed = (codes[0] + codes[2]) + (codes[1] + codes[3])
    pseudo = summed / block_scale / len(codes)
    outer_now, moment_now, local_now = (
        pick(both, fragment, blocks) for both in (outer_params, outer_momentum, local_params)
    )
    outer_new, moment_new = nesterov_update(outer_now, moment_now, pseudo)
    merged = mixing_alpha * local_now + (1.0 - mixing_alpha) * outer_new
    return (
        put(outer_params, fragment, outer_new),
        put(outer_momentum, fragment, moment_new),
        put(local_params, fragment, merged)[None],
    )


def on_device(
    normed_input,
    kv_cotangent,
    kv_weight,
    adam_m,
    adam_v,
    outer_params,
    local_params,
    outer_momentum,
    fragment,
    block_exponent,
):
    inputs_here, cotangent_here = normed_input[0], kv_cotangent[0]
    rows = kv_weight.shape[1]
    chips, cores = lax.axis_size(("z", "y", "x")), lax.axis_size("core")
    norm_factor = math.sqrt(inputs_here.shape[0] * chips * cores)
    nx = lax.axis_size("x")
    block_scale = jnp.exp2(block_exponent.astype(jnp.float32))[:, None]
    encoded = encode(outer_params, local_params[0], fragment, block_scale)
    leaving, staying = product_by_core(inputs_here, cotangent_here, rows)
    arrived = lax.ppermute(leaving, "core", [(0, 1), (1, 0)])
    packed = packed_by_owner(fetched(staying), arrived, nx)
    pieces = lax.all_to_all(packed, "x", 0, 0, tiled=True)
    encoded = later(encoded, packed)
    islands = lax.axis_size("island")
    codes = [encoded] + [
        lax.ppermute(encoded, "island", [(i, (i + step) % islands) for i in range(islands)])
        for step in range(1, islands)
    ]
    total, codes = lax.optimization_barrier((total_of(pieces), codes))
    gathered = lax.all_to_all(
        total.reshape(chips // nx, rows, -1), ("z", "y"), 0, 0, tiled=True
    )
    outer_result = outer_step(
        codes, outer_params, local_params[0], outer_momentum, fragment, block_scale
    )
    gradient = jnp.sum(gathered.astype(jnp.float32), axis=0) / norm_factor
    inner_result = adamw_step(kv_weight[0], adam_m[0], adam_v[0], gradient)
    return tuple(part[None] for part in inner_result) + outer_result


def solution(mesh):
    grid = Mesh(mesh.devices.reshape(mesh.shape["island"], 3, 8, 4, 2), ("island",) + FSDP)
    in_specs = (
        P("island", FSDP, None),
        P("island", FSDP, None),
        P("island", FSDP, None),
        P("island", FSDP, None),
        P("island", FSDP, None),
        P(None, FSDP),
        P("island", None, FSDP),
        P(None, FSDP),
        P(),
        P(FSDP),
    )
    out_specs = (
        P("island", FSDP, None),
        P("island", FSDP, None),
        P("island", FSDP, None),
        P(None, FSDP),
        P(None, FSDP),
        P("island", None, FSDP),
    )
    return jax.shard_map(
        on_device, mesh=grid, in_specs=in_specs, out_specs=out_specs, check_vma=False
    )
```
